128 devices in a mesh: dp: 8 (over x, core), tensor: 16 (over y, z).
Axes of the slice: x: 4, y: 4, z: 4, core: 2. Of those that a mesh axis runs over, the one named last changes fastest.
Arguments:
- stream: bfloat16 [16, 4, 8192], P('dp', None, 'tensor'), may hold values from -6 to 6
- norm_gain: bfloat16 [8192], P('tensor'), may hold values from 0.5 to 1.5
- w_q: bfloat16 [8192, 64, 128], P(None, 'tensor'), may hold values from -0.0625 to 0.0625
- w_kv: bfloat16 [8192, 16, 256], P(None, 'tensor'), as said below
- w_o: bfloat16 [64, 128, 8192], P('tensor'), may hold values from -0.0625 to 0.0625
- prefix_kv: bfloat16 [4, 2048, 16, 256], P(None, 'dp', 'tensor'), may hold values from -620 to 620, as said below
- prompt_len: int32 [4], replicated, may hold values from 512 to 2048, as said below
- suffix_kv: bfloat16 [16, 4, 256, 16, 256], P('dp', None, None, 'tensor'), may hold values from -6 to 6, as said below
- suffix_len: int32 [16, 4], replicated, may hold values from 0 to 255, as said below
- log_weight: float32 [16, 4], P('dp'), may hold values from -12 to 412
- potential: bfloat16 [8192], P('tensor'), may hold values from -0.0625 to 0.0625
- anc_group: int32 [16, 4, 1], replicated, may hold values from 0 to 7; in each aligned block of 8 rows (0 to 7, 8 to 15, ..., all dimensions but the last counted through in order) at most 2 rows name the same one
- anc_member: int32 [16, 4], replicated, may hold values from 0 to 1
Outputs:
- mixed: bfloat16 [16, 4, 8192], P('dp', None, 'tensor')
- normalized: float32 [16, 4], P('dp')
- new_suffix: bfloat16 [16, 4, 256, 16, 256], P('dp', None, None, 'tensor')
The draws below stay inside these ranges and needn't reach their ends.
Inputs may be any that keep to these rules, and one draw needn't show every extreme that they name: Ancestor particle of particle p in prompt q is 2 * anc_group[p, q, 0] + anc_member[p, q]. Among the rows of one block (8 rows in order, particle-major), at most 2 name one block, and some block is named by exactly 2 of them. `prompt_len`: some prompt has all 2048 positions. `suffix_len`: some particle has 255. `w_kv`: copies 2 k and 2 k + 1 along the middle dimension are equal; both hold key head k. `prefix_kv`: copies 2 k and 2 k + 1 along the third dimension are equal; both hold key head k. `suffix_kv`: copies 2 k and 2 k + 1 along the fourth dimension are equal; both hold key head k.
All inputs are finite; a program needn't handle non-finite values.
Results may differ from the reference program's by a relative error of at most 0.011.
Values may be sent and summed in bfloat16 or wider, within the bound.
A program may use at most 128 MiB of HBM per device.

```python
import math
import jax
import jax.numpy as jnp
import numpy as np
from jax import lax

D = 8192
HEADS = 64
KVH = 8
HD = 128
PARTICLES = 16
PROMPTS = 4
LP = 2048
LS = 256
PER_COPY = 4
SLOTS = 2
CAP = 2
N_DP = 8


def doubled(values):
    lead = values.shape[:-2]
    twice = jnp.stack([values, values], axis=-2)
    return twice.reshape(lead + (2 * values.shape[-2], values.shape[-1]))


def draw_w_kv(key, part):
    key = jax.random.fold_in(key, 11)
    values = jnp.clip(jax.random.normal(key, (D, KVH, 2 * HD), jnp.float32), -6.0, 6.0) * D ** (-0.5)
    return doubled(values).astype(jnp.bfloat16)


def draw_suffix_kv(key, part):
    key = jax.random.fold_in(key, 13)
    values = jnp.clip(jax.random.normal(key, (PARTICLES, PROMPTS, LS, KVH, 2 * HD), jnp.float32), -6.0, 6.0)
    return doubled(values).astype(jnp.bfloat16)


def draw_prefix_kv(key, part):
    key = jax.random.fold_in(key, 15)
    key_base = jax.random.fold_in(key, 0)
    values = jnp.clip(jax.random.normal(key_base, (PROMPTS, LP, KVH, 2 * HD), jnp.float32), -6.0, 6.0)
    return doubled(values).astype(jnp.bfloat16)


def draw_prompt_len(key, part):
    key = jax.random.fold_in(key, 5)
    key_lengths, key_chosen = jax.random.split(key)
    lengths = jax.random.randint(key_lengths, (PROMPTS,), LP // 4, LP + 1)
    chosen = jax.random.randint(key_chosen, (), 0, PROMPTS)
    return jnp.where(jnp.arange(PROMPTS) == chosen, LP, lengths).astype(jnp.int32)


def draw_suffix_len(key, part):
    key = jax.random.fold_in(key, 7)
    key_lengths, key_chosen = jax.random.split(key)
    lengths = jax.random.randint(key_lengths, (PARTICLES, PROMPTS), 0, LS)
    chosen = jax.random.randint(key_chosen, (), 0, PARTICLES * PROMPTS)
    flat_index = jnp.arange(PARTICLES * PROMPTS).reshape(PARTICLES, PROMPTS)
    return jnp.where(flat_index == chosen, LS - 1, lengths).astype(jnp.int32)


def draw_log_weight(key, part):
    key = jax.random.fold_in(key, 9)
    key_noise = jax.random.fold_in(key, 1)
    values = 3.0 * jax.random.normal(key_noise, (PARTICLES, PROMPTS), jnp.float32)
    return jnp.clip(values, -12.0, 12.0).astype(jnp.float32)


def place_ends(result, rng, low, largest):
    spot = [jax.random.randint(jax.random.fold_in(rng, axis), (), 0, length) for axis, length in enumerate(result.shape)]
    main_axis = result.shape.index(max(result.shape))
    beside = spot[:main_axis] + [(spot[main_axis] + 1) % result.shape[main_axis]] + spot[main_axis + 1:]
    return result.at[tuple(spot)].set(low).at[tuple(beside)].set(largest)


def block_scale(stream_key, extent, cuts, low, largest):
    def one(dim, shards_of):
        draws = jax.random.uniform(jax.random.fold_in(jax.random.fold_in(stream_key, 6), dim), (shards_of,), jnp.float32, low / len(cuts), largest / len(cuts))
        return jnp.repeat(jnp.exp(draws), extent[dim] // shards_of).reshape((-1,) + (1,) * (len(extent) - dim - 1))

    factor_of = one(*cuts[0])
    for cut in cuts[1:]:
        factor_of = factor_of * one(*cut)
    return factor_of


def routed_block(own_key, own, number, rows, amount, top, limit, slope):
    sequence = jax.random.permutation(own_key, amount)
    heavy_load, usual = portions_of(amount, rows * top, limit, slope, True), portions_of(amount, rows * top, limit, slope, False)
    places = jnp.arange(amount)

    def named(tallies, offset_by):
        used = int((tallies > 0).sum())
        fixed = max(1, used // 4)
        shifted = fixed + (places - fixed + offset_by * (used - fixed)) % max(1, amount - fixed)
        return jnp.zeros((amount,), jnp.int32).at[sequence[jnp.where(places < fixed, places, shifted)]].set(jnp.asarray(tallies, jnp.int32))

    tallies = jnp.where(number % 4 == 0, named(heavy_load, number // 4), named(usual, number - number // 4 - 1))
    mixed = jax.random.permutation(jax.random.fold_in(own, 3), amount)
    source_of, sink = mixed[0:amount // 2 * 2:2], mixed[1:amount // 2 * 2:2]
    margin = jnp.minimum(tallies[source_of] - 1, limit - tallies[sink]) // 2
    margin = jnp.where((source_of == sequence[0]) | (sink == sequence[0]) | (tallies[sink] == 0), 0, jnp.maximum(margin, 0))
    shifted = jax.random.randint(jax.random.fold_in(own, 4), (amount // 2,), 0, 1 << 20) % (margin + 1)
    tallies = tallies.at[source_of].add(-shifted).at[sink].add(shifted)
    items = jnp.searchsorted(jnp.cumsum(tallies), jnp.arange(rows * top), side="right").astype(jnp.int32)
    table = items.reshape(top, rows).T
    table = table[jax.random.permutation(jax.random.fold_in(own, 1), rows)]
    offset_by = jax.random.randint(jax.random.fold_in(own, 2), (rows, 1), 0, top)
    return jnp.take_along_axis(table, (jnp.arange(top)[None, :] + offset_by) % top, axis=1)


def portions_of(number_of, total, most, slope, full):
    weights = [(1 << 20) // math.isqrt(standing ** slope) + 1 for standing in range(1, number_of + 1)]
    largest = most if full else min(most, max(-(-total // number_of), total * weights[0] // sum(weights)))
    least = 1 if total - largest >= number_of - 1 else 0
    counts, surplus = [largest] + [least] * (number_of - 1), total - largest - least * (number_of - 1)
    while surplus > 0:
        candidates = [i for i in range(1, number_of) if counts[i] < largest] or [i for i in range(1, number_of) if counts[i] < most]
        whole, remaining = sum([weights[i] for i in candidates]), surplus
        for i in candidates:
            addition = min(most - counts[i], max(1, remaining * weights[i] // whole), surplus)
            counts[i] = counts[i] + addition
            surplus = surplus - addition
    return np.array(counts)


def normal_values(own_key, dims, width, reach, shards=(), kind=jnp.bfloat16):
    entries = jax.random.normal(own_key, dims, jnp.float32) * width
    if len(shards) > 0:
        entries = block_scale(own_key, dims, shards, -0.22, 0.18) * entries
    return jnp.clip(entries, min=-reach, max=reach).astype(kind)


def setup_inputs(seed: int = 0) -> dict:
    arg_keys = jax.random.split(jax.random.key(seed), 14)
    stream = normal_values(arg_keys[0], (PARTICLES, PROMPTS, D), 1.0, 6.0, ((0, 8), (2, 16)))
    norm_gain = jnp.clip(1.0 + 0.1 * jax.random.normal(arg_keys[1], (D,), jnp.float32), 0.5, 1.5).astype(jnp.bfloat16)
    w_q = normal_values(arg_keys[2], (D, HEADS, HD), D ** -0.5, 0.0625, ((1, 16),))
    w_kv = draw_w_kv(jax.random.fold_in(arg_keys[13], 71), 0)
    w_o = normal_values(arg_keys[4], (HEADS, HD, D), (HEADS * HD) ** -0.5, 0.0625, ((0, 16),))
    prefix_kv = draw_prefix_kv(jax.random.fold_in(arg_keys[13], 71), 0)
    prompt_len = draw_prompt_len(jax.random.fold_in(arg_keys[13], 71), 0)
    suffix_kv = draw_suffix_kv(jax.random.fold_in(arg_keys[13], 71), 0)
    suffix_len = draw_suffix_len(jax.random.fold_in(arg_keys[13], 71), 0)
    log_weight = draw_log_weight(jax.random.fold_in(arg_keys[13], 71), 0)
    potential = normal_values(arg_keys[10], (D,), D ** -0.5, 0.0625, ((0, 16),))
    anc_group_keys = jax.random.split(jax.random.fold_in(arg_keys[11], 1), PARTICLES * PROMPTS // (SLOTS * PROMPTS))
    anc_group_turns = jax.random.permutation(jax.random.fold_in(arg_keys[11], 3), PARTICLES * PROMPTS // (SLOTS * PROMPTS))
    anc_group = jax.vmap(lambda own, number: routed_block(jax.random.fold_in(arg_keys[11], 2), own, number, SLOTS * PROMPTS, N_DP, 1, CAP, 2))(anc_group_keys, anc_group_turns).reshape((PARTICLES, PROMPTS, 1))
    anc_member = place_ends(jax.random.randint(arg_keys[12], (PARTICLES, PROMPTS), 0, SLOTS), jax.random.fold_in(arg_keys[12], 1), 0, SLOTS - 1).astype(jnp.int32)
    return {"stream": stream, "norm_gain": norm_gain, "w_q": w_q, "w_kv": w_kv, "w_o": w_o, "prefix_kv": prefix_kv, "prompt_len": prompt_len, "suffix_kv": suffix_kv, "suffix_len": suffix_len, "log_weight": log_weight, "potential": potential, "anc_group": anc_group, "anc_member": anc_member}


def reference(stream, norm_gain, w_q, w_kv, w_o, prefix_kv, prompt_len, suffix_kv, suffix_len, log_weight, potential, anc_group, anc_member):
    xfloat = stream.astype(jnp.float32)
    meansq = lax.optimization_barrier(jnp.mean(xfloat * xfloat, axis=-1, keepdims=True))
    normed = (xfloat * lax.rsqrt(meansq + 1e-05) * norm_gain.astype(jnp.float32)).astype(jnp.bfloat16)
    flattened = normed.reshape(PARTICLES * PROMPTS, D)
    queries = (jnp.dot(flattened, w_q.reshape(D, HEADS * HD), preferred_element_type=jnp.float32) * HD ** (-0.5)).astype(jnp.bfloat16)
    queries = queries.reshape(PARTICLES, PROMPTS, 2 * KVH, PER_COPY, HD).astype(jnp.float32)
    fresh = jnp.dot(flattened, w_kv.reshape(D, 2 * KVH * 2 * HD), preferred_element_type=jnp.float32).astype(jnp.bfloat16)
    fresh = fresh.reshape(PARTICLES, PROMPTS, 2 * KVH, 2 * HD)
    places = jnp.arange(LS, dtype=jnp.int32)
    landing = places[None, None, :] == suffix_len[:, :, None]
    appended = jnp.where(landing[:, :, :, None, None], fresh[:, :, None], suffix_kv)
    pre_keys = prefix_kv[..., :HD].astype(jnp.float32)
    pre_values = prefix_kv[..., HD:].astype(jnp.float32)
    suf_keys = appended[..., :HD].astype(jnp.float32)
    suf_values = appended[..., HD:].astype(jnp.float32)
    pre_scores = jnp.einsum('pqcgd,qlcd->pqcgl', queries, pre_keys)
    suf_scores = jnp.einsum('pqcgd,pqlcd->pqcgl', queries, suf_keys)
    pre_mask = jnp.arange(LP, dtype=jnp.int32)[None, :] < prompt_len[:, None]
    suf_mask = places[None, None, :] <= suffix_len[:, :, None]
    pre_scores = jnp.where(pre_mask[None, :, None, None, :], pre_scores, -jnp.inf)
    suf_scores = jnp.where(suf_mask[:, :, None, None, :], suf_scores, -jnp.inf)
    highest = jnp.maximum(lax.optimization_barrier(jnp.max(pre_scores, axis=-1)), lax.optimization_barrier(jnp.max(suf_scores, axis=-1)))
    pre_exp = jnp.exp(pre_scores - highest[..., None])
    suf_exp = jnp.exp(suf_scores - highest[..., None])
    totals = lax.optimization_barrier(jnp.sum(pre_exp, axis=-1)) + lax.optimization_barrier(jnp.sum(suf_exp, axis=-1))
    pre_probs = (pre_exp / totals[..., None]).astype(jnp.bfloat16).astype(jnp.float32)
    suf_probs = (suf_exp / totals[..., None]).astype(jnp.bfloat16).astype(jnp.float32)
    attended = jnp.einsum('pqcgl,qlcd->pqcgd', pre_probs, pre_values)
    attended = attended + jnp.einsum('pqcgl,pqlcd->pqcgd', suf_probs, suf_values)
    attended = attended.astype(jnp.bfloat16).reshape(PARTICLES * PROMPTS, HEADS * HD)
    projected = jnp.dot(attended, w_o.reshape(HEADS * HD, D), preferred_element_type=jnp.float32)
    mixed = (xfloat + projected.reshape(PARTICLES, PROMPTS, D)).astype(jnp.bfloat16)
    updated = log_weight + lax.optimization_barrier(jnp.sum(mixed.astype(jnp.float32) * potential.astype(jnp.float32), axis=-1))
    weight_top = lax.optimization_barrier(jnp.max(updated, axis=0))
    log_total = weight_top + jnp.log(lax.optimization_barrier(jnp.sum(jnp.exp(updated - weight_top[None, :]), axis=0)))
    normalized = updated - log_total[None, :]
    ancestor = anc_group[:, :, 0] * SLOTS + anc_member
    new_suffix = appended[ancestor, jnp.arange(PROMPTS, dtype=jnp.int32)[None, :]]
    return (mixed, normalized, new_suffix)
```

```python
import functools

import jax
import jax.numpy as jnp
from jax import lax
from jax.experimental import pallas as pl
from jax.experimental.pallas import tpu as pltpu
from jax.sharding import PartitionSpec as P

MESH = pl.DeviceIdType.MESH
F32 = jnp.float32
BF16 = jnp.bfloat16
LOW = -1e30


def dot(a, b):
    return jnp.dot(a, b, preferred_element_type=F32)


def dot_t(a, b):
    return lax.dot_general(a, b, (((1,), (1,)), ((), ())), preferred_element_type=F32)


def step_kernel(
    n_dp,
    n_t,
    stream_ref,
    gain_ref,
    pot_ref,
    wq_hbm,
    wkv_hbm,
    wo_hbm,
    pre_hbm,
    suf_hbm,
    plen_ref,
    slen_ref,
    lw_ref,
    group_ref,
    member_ref,
    mixed_ref,
    norm_ref,
    new_hbm,
    wq,
    wkv,
    wo,
    pre,
    suf,
    block_out,
    block_in,
    new,
    x_out,
    x_in,
    qkv_out,
    qkv_in,
    att_out,
    att_in,
    proj_out,
    proj_in,
    part_out,
    part_in,
    upd_out,
    upd_in,
    local_sem,
    new_sem,
    block_ssem,
    block_rsem,
    x_ssem,
    x_rsem,
    qkv_ssem,
    qkv_rsem,
    att_ssem,
    att_rsem,
    proj_ssem,
    proj_rsem,
    part_ssem,
    part_rsem,
    upd_ssem,
    upd_rsem,
):
    me = lax.axis_index("dp")
    mt = lax.axis_index("tensor")

    def dp_peer(k):
        return lax.rem(me + k, n_dp)

    def t_peer(k):
        return lax.rem(mt + k, n_t)

    def to_dp(src, dst, ssem, rsem, k):
        return pltpu.make_async_remote_copy(
            src_ref=src, dst_ref=dst, send_sem=ssem, recv_sem=rsem,
            device_id=(dp_peer(k), mt), device_id_type=MESH,
        )

    def to_t(src, dst, ssem, rsem, k):
        return pltpu.make_async_remote_copy(
            src_ref=src, dst_ref=dst, send_sem=ssem, recv_sem=rsem,
            device_id=(me, t_peer(k)), device_id_type=MESH,
        )

    def each(n, body):
        def run(k, carry):
            body(k)
            return carry

        lax.fori_loop(1, n, run, 0)

    load_suf = pltpu.make_async_copy(suf_hbm, suf, local_sem.at[0])
    load_wq = pltpu.make_async_copy(wq_hbm, wq, local_sem.at[1])
    load_wkv = pltpu.make_async_copy(wkv_hbm, wkv, local_sem.at[2])
    load_pre = pltpu.make_async_copy(pre_hbm, pre, local_sem.at[3])
    load_suf.start()
    load_wq.start()
    load_wkv.start()
    load_pre.start()
    width = wo.shape[2]
    load_wo = [
        pltpu.make_async_copy(
            wo_hbm.at[:, pl.ds(c * width, width)], wo.at[c], local_sem.at[4 + c]
        )
        for c in range(n_t)
    ]
    for c in range(n_t):
        load_wo[c].start()

    barrier = pltpu.get_barrier_semaphore()
    each(n_t, lambda k: pl.semaphore_signal(
        barrier, inc=1, device_id=(me, t_peer(k)), device_id_type=MESH))
    each(n_dp, lambda k: pl.semaphore_signal(
        barrier, inc=1, device_id=(dp_peer(k), mt), device_id_type=MESH))
    pl.semaphore_wait(barrier, n_t + n_dp - 2)

    x0 = stream_ref[0].astype(F32)
    x1 = stream_ref[1].astype(F32)
    x_own = jnp.concatenate([x0, x1], axis=0)
    half = width // 2
    gain_row = gain_ref[...].astype(F32).reshape(1, width)
    pot_row = pot_ref[...].astype(F32).reshape(1, width)
    rows = [gain_row[:, c * 128:(c + 1) * 128] for c in range(4)]
    rows += [pot_row[:, c * 128:(c + 1) * 128] for c in range(4)]
    vectors = jnp.concatenate(rows, axis=0)
    x_out[:, :half] = jnp.concatenate([x_own[:, :half], x_own[:, half:]], axis=0).astype(BF16)
    x_out[:, half:] = jnp.concatenate([vectors, vectors], axis=0).astype(BF16)

    def send_x(k):
        to_t(x_out, x_in.at[mt], x_ssem.at[k - 1], x_rsem.at[k - 1], k).start()

    each(n_t, send_x)
    x_in[mt] = x_out[...]

    load_suf.wait()

    def choose(j):
        first = jnp.int32(0)
        second = jnp.int32(0)
        count = jnp.int32(0)
        for p in range(2):
            for q in range(4):
                hit = group_ref[q, 2 * j + p] == me
                at = member_ref[q, 2 * j + p] * 4 + q
                first = jnp.where(hit & (count == 0), at, first)
                second = jnp.where(hit & (count == 1), at, second)
                count = count + hit.astype(jnp.int32)
        return first, second

    def send_blocks(k):
        first, second = choose(dp_peer(k))
        block_out[k - 1, 0] = suf[first]
        block_out[k - 1, 1] = suf[second]
        to_dp(block_out.at[k - 1], block_in.at[me], block_ssem.at[k - 1], block_rsem.at[k - 1], k).start()

    each(n_dp, send_blocks)
    first, second = choose(me)
    block_in[me, 0] = suf[first]
    block_in[me, 1] = suf[second]

    lane512 = lax.broadcasted_iota(jnp.int32, (8, 512), 1)
    spread_r = lax.broadcasted_iota(jnp.int32, (128, 512), 0)
    spread_c = lax.broadcasted_iota(jnp.int32, (128, 512), 1)
    spread = jnp.where(spread_c // 4 == spread_r, 1.0, 0.0).astype(BF16)

    def wait_x(k):
        to_t(x_out, x_in.at[t_peer(n_t - k)], x_ssem.at[k - 1], x_rsem.at[k - 1], k).wait_recv()

    each(n_t, wait_x)
    squares = jnp.zeros((16, half), F32)
    for c in range(n_t):
        part = x_in[c, :, :half].astype(F32)
        squares = squares + part * part
    squares = squares[:8] + squares[8:]
    scale = lax.rsqrt(jnp.sum(squares, axis=1, keepdims=True) * (1.0 / (width * n_t)) + 1e-05)
    load_wkv.wait()
    load_wq.wait()
    q_acc = jnp.zeros((32, 128), F32)
    kv_acc = jnp.zeros((8, 256), F32)
    for c in range(n_t):
        part = x_in[c, :, :half].astype(F32)
        part = jnp.concatenate([part[:8], part[8:]], axis=1)
        gains = x_in[c, :, half:].astype(F32)
        gain = jnp.concatenate([gains[r:r + 1] for r in range(4)], axis=1)
        normed = (part * scale * gain).astype(BF16)
        kv_acc = kv_acc + dot(normed, wkv[c * width:(c + 1) * width, :])
        for b in range(4):
            wide = dot(normed[:, b * 128:(b + 1) * 128], spread)
            lhs = jnp.concatenate(
                [jnp.where(lane512 % 4 == h, wide, 0.0) for h in range(4)], axis=0
            ).astype(BF16)
            start = (c * 4 + b) * 512
            q_acc = q_acc + dot(lhs, wq[start:start + 512, :])

    row = lax.broadcasted_iota(jnp.int32, (32, 32), 0)
    col = lax.broadcasted_iota(jnp.int32, (32, 32), 1)
    source = (row % 4) * 8 + ((row // 4) % 2) * 4 + row // 8
    turn = jnp.where(col == source, 1.0, 0.0).astype(BF16)
    q_rows = dot(turn, (q_acc * (128 ** -0.5)).astype(BF16))
    qkv_out[0:32, :] = q_rows.astype(BF16)
    qkv_out[32:48, :] = jnp.concatenate([kv_acc[:, :128], kv_acc[:, 128:]], axis=0).astype(BF16)

    def send_qkv(k):
        to_dp(qkv_out, qkv_in.at[me], qkv_ssem.at[k - 1], qkv_rsem.at[k - 1], k).start()

    each(n_dp, send_qkv)
    qkv_in[me] = qkv_out[...]

    place = lax.broadcasted_iota(jnp.int32, (256, 1), 0)
    place_row = lax.broadcasted_iota(jnp.int32, (8, 256), 1)
    second_half = lax.broadcasted_iota(jnp.int32, (8, 1), 0) >= 4
    fresh = qkv_out[32:48, :].astype(F32)
    suf_top, suf_total, suf_att = [], [], []
    for q in range(4):
        q_tile = q_rows[q * 8:(q + 1) * 8].astype(BF16)
        scores, values = [], []
        for p in range(2):
            tok = p * 4 + q
            length = slen_ref[q, 2 * me + p]
            keys = suf[tok, :, :128].astype(F32)
            vals = suf[tok, :, 128:].astype(F32)
            keys = jnp.where(place == length, fresh[tok:tok + 1], keys).astype(BF16)
            vals = jnp.where(place == length, fresh[8 + tok:9 + tok], vals).astype(BF16)
            s = dot_t(q_tile, keys)
            scores.append(jnp.where(place_row <= length, s, LOW))
            values.append(vals)
        s = jnp.where(second_half, scores[1], scores[0])
        top = jnp.max(s, axis=1, keepdims=True)
        e = jnp.exp(s - top)
        suf_top.append(top)
        suf_total.append(jnp.sum(e, axis=1, keepdims=True))
        e16 = e.astype(BF16)
        suf_att.append(jnp.where(second_half, dot(e16, values[1]), dot(e16, values[0])))

    for c in range(n_t):
        load_wo[c].wait()
    probe = jnp.zeros((8, width), F32)
    for c in range(n_t):
        vec = x_in[c, :, half:].astype(F32)
        pots = jnp.concatenate([vec[4 + r:5 + r] for r in range(4)], axis=1)
        pots = jnp.broadcast_to(pots, (8, width)).astype(BF16)
        probe = probe + dot_t(pots, wo[c])

    load_pre.wait()

    def wait_qkv(k):
        to_dp(qkv_out, qkv_in.at[dp_peer(n_dp - k)], qkv_ssem.at[k - 1], qkv_rsem.at[k - 1], k).wait_recv()

    each(n_dp, wait_qkv)
    lane8 = lax.broadcasted_iota(jnp.int32, (64, 128), 1)
    q_all = [qkv_in[j, 0:32, :].astype(F32) for j in range(n_dp)]
    place_pre = lax.broadcasted_iota(jnp.int32, (64, 256), 1) + me * 256
    stats = jnp.zeros((64, 128), F32)
    for q in range(4):
        q_mat = jnp.concatenate([q_all[j][q * 8:(q + 1) * 8] for j in range(n_dp)], axis=0).astype(BF16)
        valid = place_pre < plen_ref[q]
        s = jnp.where(valid, dot_t(q_mat, pre[q, :, :128]), LOW)
        top = jnp.max(s, axis=1, keepdims=True)
        e = jnp.where(valid, jnp.exp(s - top), 0.0)
        total = jnp.sum(e, axis=1, keepdims=True)
        o = dot(e.astype(BF16), pre[q, :, 128:])
        for j in range(n_dp):
            att_out[j, q * 8:(q + 1) * 8, :] = o[j * 8:(j + 1) * 8]
        stats = jnp.where(lane8 == q, top, stats)
        stats = jnp.where(lane8 == 4 + q, total, stats)
    for j in range(n_dp):
        att_out[j, 32:40, :] = stats[j * 8:(j + 1) * 8]

    def send_att(k):
        j = dp_peer(k)
        to_dp(att_out.at[j], att_in.at[me], att_ssem.at[k - 1], att_rsem.at[k - 1], k).start()

    each(n_dp, send_att)
    att_in[me] = att_out[me]

    def wait_att(k):
        to_dp(att_out.at[dp_peer(k)], att_in.at[dp_peer(n_dp - k)], att_ssem.at[k - 1], att_rsem.at[k - 1], k).wait_recv()

    each(n_dp, wait_att)

    lane = lax.broadcasted_iota(jnp.int32, (8, 128), 1)
    all_stats = [att_in[j, 32:40, :] for j in range(n_dp)]
    attended = []
    for q in range(4):
        tops = [st[:, q:q + 1] for st in all_stats]
        totals = [st[:, 4 + q:5 + q] for st in all_stats]
        best = suf_top[q]
        for j in range(n_dp):
            best = jnp.maximum(best, tops[j])
        factor = jnp.exp(suf_top[q] - best)
        denom = factor * suf_total[q]
        numer = factor * suf_att[q]
        for j in range(n_dp):
            factor = jnp.exp(tops[j] - best)
            denom = denom + factor * totals[j]
            numer = numer + factor * att_in[j, q * 8:(q + 1) * 8, :]
        attended.append(numer / denom)
    att_rows = jnp.concatenate(attended, axis=0).astype(BF16)
    by_head = dot(turn, att_rows)
    att_lhs = jnp.concatenate([by_head[h * 8:(h + 1) * 8] for h in range(4)], axis=1)

    part = jnp.sum(att_lhs * probe + x_own * pot_row, axis=1, keepdims=True)
    part_out[...] = jnp.broadcast_to(part, (8, 128))

    def send_part(k):
        to_t(part_out, part_in.at[mt], part_ssem.at[k - 1], part_rsem.at[k - 1], k).start()

    each(n_t, send_part)
    part_in[mt] = part_out[...]

    lhs = att_lhs.astype(BF16)

    def send_proj(k):
        t = t_peer(k)
        proj_out[k - 1] = dot(lhs, wo[t])
        to_t(proj_out.at[k - 1], proj_in.at[mt], proj_ssem.at[k - 1], proj_rsem.at[k - 1], k).start()

    each(n_t, send_proj)
    shared = dot(lhs, wo[mt])
    proj_in[mt] = shared

    def wait_part(k):
        to_t(part_out, part_in.at[t_peer(n_t - k)], part_ssem.at[k - 1], part_rsem.at[k - 1], k).wait_recv()

    each(n_t, wait_part)
    inner = part_in[0]
    for c in range(1, n_t):
        inner = inner + part_in[c]
    sub = lax.broadcasted_iota(jnp.int32, (8, 128), 0)
    weight = jnp.zeros((8, 128), F32)
    for p in range(2):
        for q in range(4):
            weight = jnp.where(sub == p * 4 + q, lw_ref[p, q], weight)
    updated = weight + inner
    upd_out[...] = updated

    def send_upd(k):
        to_dp(upd_out, upd_in.at[me], upd_ssem.at[k - 1], upd_rsem.at[k - 1], k).start()

    each(n_dp, send_upd)
    upd_in[me] = updated

    def wait_blocks(k):
        to_dp(block_out.at[k - 1], block_in.at[dp_peer(n_dp - k)], block_ssem.at[k - 1], block_rsem.at[k - 1], k).wait_recv()

    each(n_dp, wait_blocks)
    row16 = lax.broadcasted_iota(jnp.int32, (16, 128), 0)
    named = []
    for p in range(2):
        for q in range(4):
            tok = p * 4 + q
            g = group_ref[q, 2 * me + p]
            m = member_ref[q, 2 * me + p]
            slot = jnp.int32(0)
            for other in named:
                slot = slot + (other == g).astype(jnp.int32)
            named.append(g)
            length = slen_ref[q, 2 * g + m]
            line = qkv_in[g, 32:48, :].astype(F32)
            line_k = jnp.sum(jnp.where(row16 == m * 4 + q, line, 0.0), axis=0, keepdims=True)
            line_v = jnp.sum(jnp.where(row16 == 8 + m * 4 + q, line, 0.0), axis=0, keepdims=True)
            line = jnp.concatenate([line_k, line_v], axis=1)
            block = block_in[g, jnp.minimum(slot, 1)].astype(F32)
            new[tok] = jnp.where(place == length, line, block).astype(BF16)
            pltpu.make_async_copy(new.at[tok], new_hbm.at[tok], new_sem.at[tok]).start()

    def wait_proj(k):
        to_t(proj_out.at[k - 1], proj_in.at[t_peer(n_t - k)], proj_ssem.at[k - 1], proj_rsem.at[k - 1], k).wait_recv()

    each(n_t, wait_proj)
    shared = proj_in[0]
    for c in range(1, n_t):
        shared = shared + proj_in[c]
    mixed = x_own + shared
    mixed_ref[0] = mixed[:4].astype(BF16)
    mixed_ref[1] = mixed[4:].astype(BF16)

    def wait_upd(k):
        to_dp(upd_out, upd_in.at[dp_peer(n_dp - k)], upd_ssem.at[k - 1], upd_rsem.at[k - 1], k).wait_recv()

    each(n_dp, wait_upd)
    everyone = [upd_in[j] for j in range(n_dp)]
    best = everyone[0]
    for j in range(1, n_dp):
        best = jnp.maximum(best, everyone[j])
    best = jnp.maximum(best, jnp.concatenate([best[4:], best[:4]], axis=0))
    total = jnp.zeros((8, 128), F32)
    for j in range(n_dp):
        total = total + jnp.exp(everyone[j] - best)
    total = total + jnp.concatenate([total[4:], total[:4]], axis=0)
    normalized = updated - (best + jnp.log(total))
    picked = jnp.where(sub % 4 == lane, normalized, 0.0)
    norm_ref[...] = jnp.concatenate(
        [jnp.sum(picked[:4], axis=0, keepdims=True), jnp.sum(picked[4:], axis=0, keepdims=True)], axis=0
    )[:, :4]

    for tok in range(8):
        pltpu.make_async_copy(new.at[tok], new_hbm.at[tok], new_sem.at[tok]).wait()

    def done_dp(k):
        to_dp(block_out.at[k - 1], block_in.at[me], block_ssem.at[k - 1], block_rsem.at[k - 1], k).wait_send()
        to_dp(qkv_out, qkv_in.at[me], qkv_ssem.at[k - 1], qkv_rsem.at[k - 1], k).wait_send()
        to_dp(att_out.at[dp_peer(k)], att_in.at[me], att_ssem.at[k - 1], att_rsem.at[k - 1], k).wait_send()
        to_dp(upd_out, upd_in.at[me], upd_ssem.at[k - 1], upd_rsem.at[k - 1], k).wait_send()

    def done_t(k):
        to_t(x_out, x_in.at[mt], x_ssem.at[k - 1], x_rsem.at[k - 1], k).wait_send()
        to_t(part_out, part_in.at[mt], part_ssem.at[k - 1], part_rsem.at[k - 1], k).wait_send()
        to_t(proj_out.at[k - 1], proj_in.at[mt], proj_ssem.at[k - 1], proj_rsem.at[k - 1], k).wait_send()

    each(n_dp, done_dp)
    each(n_t, done_t)


def per_device(
    n_dp,
    n_t,
    stream,
    norm_gain,
    w_q,
    w_kv,
    w_o,
    prefix_kv,
    prompt_len,
    suffix_kv,
    suffix_len,
    log_weight,
    potential,
    anc_group,
    anc_member,
):
    vmem = pl.BlockSpec(memory_space=pltpu.VMEM)
    smem = pl.BlockSpec(memory_space=pltpu.SMEM)
    hbm = pl.BlockSpec(memory_space=pl.ANY)
    dma = pltpu.SemaphoreType.DMA
    mixed, normalized, new = pl.pallas_call(
        functools.partial(step_kernel, n_dp, n_t),
        out_shape=(
            jax.ShapeDtypeStruct((2, 4, 512), BF16),
            jax.ShapeDtypeStruct((2, 4), F32),
            jax.ShapeDtypeStruct((8, 256, 256), BF16),
        ),
        in_specs=[vmem, vmem, vmem, hbm, hbm, hbm, hbm, hbm, smem, smem, smem, smem, smem],
        out_specs=(vmem, vmem, hbm),
        scratch_shapes=[
            pltpu.VMEM((32768, 128), BF16),
            pltpu.VMEM((8192, 256), BF16),
            pltpu.VMEM((n_t, 512, 512), BF16),
            pltpu.VMEM((4, 256, 256), BF16),
            pltpu.VMEM((8, 256, 256), BF16),
            pltpu.VMEM((n_dp - 1, 2, 256, 256), BF16),
            pltpu.VMEM((n_dp, 2, 256, 256), BF16),
            pltpu.VMEM((8, 256, 256), BF16),
            pltpu.VMEM((16, 384), BF16),
            pltpu.VMEM((n_t, 16, 384), BF16),
            pltpu.VMEM((48, 128), BF16),
            pltpu.VMEM((n_dp, 48, 128), BF16),
            pltpu.VMEM((n_dp, 40, 128), F32),
            pltpu.VMEM((n_dp, 40, 128), F32),
            pltpu.VMEM((n_t - 1, 8, 512), F32),
            pltpu.VMEM((n_t, 8, 512), F32),
            pltpu.VMEM((8, 128), F32),
            pltpu.VMEM((n_t, 8, 128), F32),
            pltpu.VMEM((8, 128), F32),
            pltpu.VMEM((n_dp, 8, 128), F32),
            dma((4 + n_t,)),
            dma((8,)),
            dma((n_dp - 1,)),
            dma((n_dp - 1,)),
            dma((n_t - 1,)),
            dma((n_t - 1,)),
            dma((n_dp - 1,)),
            dma((n_dp - 1,)),
            dma((n_dp - 1,)),
            dma((n_dp - 1,)),
            dma((n_t - 1,)),
            dma((n_t - 1,)),
            dma((n_t - 1,)),
            dma((n_t - 1,)),
            dma((n_dp - 1,)),
            dma((n_dp - 1,)),
        ],
        compiler_params=pltpu.CompilerParams(
            collective_id=0, has_side_effects=True, vmem_limit_bytes=48 * 1024 * 1024
        ),
    )(
        stream,
        norm_gain,
        potential,
        w_q.reshape(32768, 128),
        w_kv.reshape(8192, 256),
        w_o.reshape(512, 8192),
        prefix_kv.reshape(4, 256, 256),
        suffix_kv.reshape(8, 256, 256),
        prompt_len,
        suffix_len.T,
        log_weight,
        anc_group[:, :, 0].T,
        anc_member.T,
    )
    return mixed, normalized, new.reshape(2, 4, 256, 1, 256)


def solution(mesh):
    placed = (
        P("dp", None, "tensor"),
        P("tensor"),
        P(None, "tensor", None),
        P(None, "tensor", None),
        P("tensor", None, None),
        P(None, "dp", "tensor", None),
        P(),
        P("dp", None, None, "tensor", None),
        P(),
        P("dp", None),
        P("tensor"),
        P(),
        P(),
    )
    return jax.shard_map(
        functools.partial(per_device, mesh.shape["dp"], mesh.shape["tensor"]),
        mesh=mesh,
        in_specs=placed,
        out_specs=(P("dp", None, "tensor"), P("dp", None), P("dp", None, None, "tensor", None)),
        check_vma=False,
    )
```
